128 devices in a mesh: pair: 8 (over z, core), virt: 16 (over y, x).
Axes of the slice: x: 4, y: 4, z: 4, core: 2. Of those that a mesh axis runs over, the one named last changes fastest.
Arguments:
- amplitudes: bfloat16 [64, 2048, 2048], P('pair', 'virt'), may hold values from -6 to 6
- cycle_panel: bfloat16 [2048, 2048], P(('pair', 'virt')), may hold values from -0.125 to 0.125
- ladder_panel: bfloat16 [2048, 2048], P(('pair', 'virt')), may hold values from -0.125 to 0.125
- virt_energy: float32 [2048], replicated, may hold values from 0.5 to 8
- pair_energy: float32 [64], P('pair'), may hold values from -4 to -1
- tile_mask: int32 [64, 32, 32], P('pair', None, 'virt'), may hold values 0 or 1
Outputs:
- updated: bfloat16 [64, 2048, 2048], P('pair', None, 'virt')
The draws below stay inside these ranges and needn't reach their ends.
All inputs are finite; a program needn't handle non-finite values. No bound on the sum of `tile_mask` on one device may be relied on, other than what follows from the above.
Results may differ from the reference program's by a relative error of at most 0.004.
Values may be sent and summed in bfloat16 or wider, within the bound.
No kernel may reach another device: no remote copies, remote signals or barrier semaphores. Data moves between devices by JAX's collectives and lax.ppermute only.
A program may use at most 128 MiB of HBM per device.

```python
import math
import jax
import jax.numpy as jnp
from jax import lax

V = 2048
TILE = 64
ROWS = 64
NT = 32


def with_ends(values, own_key, least, high):
    longest = values.shape.index(max(values.shape))
    spots = []
    for shift in (0, 1):
        where = [jax.random.randint(jax.random.fold_in(own_key, axis), (), 0, length) for axis, length in enumerate(values.shape)]
        where[longest] = (where[longest] + shift) % values.shape[longest]
        spots.append(tuple(where))
    return values.at[spots[0]].set(least).at[spots[1]].set(high)


def block_scale(key, extent, cuts, smallest, largest):
    factor_of = 1.0
    for dim, shards_of in cuts:
        heights = jax.random.uniform(jax.random.fold_in(jax.random.fold_in(key, 6), dim), (shards_of,), jnp.float32, smallest / len(cuts), largest / len(cuts))
        factor_of = factor_of * jnp.repeat(jnp.exp(heights), extent[dim] // shards_of).reshape((-1,) + (1,) * (len(extent) - 1 - dim))
    return factor_of


def normal_values(key, extent, scale, most, shards=(), held_as=jnp.bfloat16):
    result = jax.random.normal(key, extent, jnp.float32) * scale
    if len(shards) > 0:
        result = block_scale(key, extent, shards, -0.22, 0.18) * result
    return jnp.clip(result, min=-most, max=most).astype(held_as)


def setup_inputs(seed: int = 0) -> dict:
    key_of = jax.random.split(jax.random.key(seed), 7)
    amplitudes = normal_values(key_of[0], (ROWS, V, V), 1.0, 6.0, ((0, 8), (1, 16)))
    cycle_panel = normal_values(key_of[1], (V, V), V ** -0.5, 0.125, ((0, 128),))
    ladder_panel = normal_values(key_of[2], (V, V), V ** -0.5, 0.125, ((0, 128),))
    virt_energy = jnp.clip(jnp.exp(jax.random.uniform(key_of[3], (V,), jnp.float32, math.log(0.5), math.log(8.0))), 0.5, 8.0)
    pair_energy = jnp.clip(-4.0 + 3.0 * jax.random.uniform(key_of[4], (ROWS,), jnp.float32) ** block_scale(key_of[4], (ROWS,), ((0, 8),), -0.2, 0.2), -4.0, -1.0)
    tile_mask = with_ends((jax.random.randint(key_of[5], (ROWS, NT, NT), 0, 4) < 3).astype(jnp.int32), jax.random.fold_in(key_of[5], 1), 0, 1)
    return dict(amplitudes=amplitudes, cycle_panel=cycle_panel, ladder_panel=ladder_panel, virt_energy=virt_energy, pair_energy=pair_energy, tile_mask=tile_mask)


def reference(amplitudes, cycle_panel, ladder_panel, virt_energy, pair_energy, tile_mask):
    def single_pair(inputs):
        single, energy, screen = inputs
        half_ladder = jnp.dot(single, ladder_panel.T, preferred_element_type=jnp.float32).astype(jnp.bfloat16)
        combined = jnp.dot(cycle_panel, single, preferred_element_type=jnp.float32)
        combined = combined + jnp.dot(ladder_panel, half_ladder, preferred_element_type=jnp.float32)
        masked = combined.reshape(NT, TILE, NT, TILE) * screen.astype(jnp.float32)[:, None, :, None]
        denominator = virt_energy[:, None] + virt_energy[None, :] - energy
        return (masked.reshape(V, V) / denominator).astype(jnp.bfloat16)

    return lax.map(single_pair, (amplitudes, pair_energy, tile_mask))
```

```python
import functools

import jax
import jax.numpy as jnp
from jax import lax
from jax.experimental import pallas as pl
from jax.experimental.pallas import tpu as pltpu
from jax.sharding import PartitionSpec as P

TILE = 64
LANES = 128
CHUNKS = 2
MIB = 1024 * 1024


def params(mib):
    return pltpu.CompilerParams(vmem_limit_bytes=mib * MIB)


def split_kernel(a_ref, out_ref):
    for k in range(out_ref.shape[0]):
        out_ref[k] = a_ref[:, :, k * LANES : (k + 1) * LANES]


def split_columns(amplitudes):
    pairs, rows, columns = amplitudes.shape
    owners = columns // LANES
    group = pairs // 2
    return pl.pallas_call(
        split_kernel,
        grid=(pairs // group,),
        in_specs=[pl.BlockSpec((group, rows, columns), lambda i: (i, 0, 0))],
        out_specs=pl.BlockSpec((owners, group, rows, LANES), lambda i: (0, i, 0, 0)),
        out_shape=jax.ShapeDtypeStruct((owners, pairs, rows, LANES), amplitudes.dtype),
        compiler_params=params(12),
        cost_estimate=pl.CostEstimate(flops=0, bytes_accessed=amplitudes.size * 4, transcendentals=0),
        name="split_columns",
    )(amplitudes)


def half_kernel(a_ref, l_ref, out_ref):
    pairs, rows, depth = a_ref.shape
    block = lax.dot_general(
        a_ref[...].reshape(pairs * rows, depth),
        l_ref[...],
        (((1,), (1,)), ((), ())),
        preferred_element_type=jnp.float32,
    ).astype(jnp.bfloat16)
    for k in range(out_ref.shape[0]):
        out_ref[k] = block[:, k * LANES : (k + 1) * LANES].reshape(pairs, rows, LANES)


def half_ladder(amplitudes, ladder, first, count):
    rows, depth = amplitudes.shape[1:]
    width = 512
    owners = ladder.shape[0] // LANES
    group = width // LANES
    return pl.pallas_call(
        half_kernel,
        grid=(ladder.shape[0] // width,),
        in_specs=[
            pl.BlockSpec((count, rows, depth), lambda i: (first // count, 0, 0)),
            pl.BlockSpec((width, depth), lambda i: (i, 0)),
        ],
        out_specs=pl.BlockSpec((group, count, rows, LANES), lambda i: (i, 0, 0, 0)),
        out_shape=jax.ShapeDtypeStruct((owners, count, rows, LANES), jnp.bfloat16),
        compiler_params=params(16),
        cost_estimate=pl.CostEstimate(
            flops=2 * count * rows * depth * ladder.shape[0],
            bytes_accessed=ladder.size * 2 + count * rows * depth * 4,
            transcendentals=0,
        ),
        name="half_ladder",
    )(amplitudes, ladder)


def widen(source, target):
    owners, count, rows, _ = source.shape
    for q in range(count // 2):
        for side in range(2):
            target[q, :, side * LANES : (side + 1) * LANES] = source[:, 2 * q + side].reshape(
                owners * rows, LANES
            )


def finish(first, total, q, energy_ref, base_ref, screen_ref, out_ref):
    height = total.shape[0]
    for side in range(2):
        r = 2 * q + side
        screen = jnp.broadcast_to(
            screen_ref[r][:, None, :], (height // TILE, TILE, LANES)
        ).reshape(height, LANES)
        masked = total[:, side * LANES : (side + 1) * LANES] * screen
        out_ref[r] = (masked / (base_ref[...] - energy_ref[first + r])).astype(out_ref.dtype)


def whole_kernel(first, energy_ref, k_ref, l_ref, a_ref, h_ref, base_ref, screen_ref, out_ref, a_wide, h_wide):
    @pl.when(pl.program_id(0) == 0)
    def _():
        widen(a_ref, a_wide)
        widen(h_ref, h_wide)

    for q in range(a_wide.shape[0]):
        total = jnp.dot(k_ref[...], a_wide[q], preferred_element_type=jnp.float32)
        total += jnp.dot(l_ref[...], h_wide[q], preferred_element_type=jnp.float32)
        finish(first, total, q, energy_ref, base_ref, screen_ref, out_ref)


def cycle_kernel(k_ref, a_ref, out_ref, a_wide):
    @pl.when(pl.program_id(0) == 0)
    def _():
        widen(a_ref, a_wide)

    for q in range(a_wide.shape[0]):
        out_ref[q] = jnp.dot(k_ref[...], a_wide[q], preferred_element_type=jnp.float32)


def ladder_kernel(first, energy_ref, l_ref, h_ref, part_ref, base_ref, screen_ref, previous_ref, out_ref, h_wide):
    del previous_ref

    @pl.when(pl.program_id(0) == 0)
    def _():
        widen(h_ref, h_wide)

    for q in range(h_wide.shape[0]):
        total = part_ref[q] + jnp.dot(l_ref[...], h_wide[q], preferred_element_type=jnp.float32)
        finish(first, total, q, energy_ref, base_ref, screen_ref, out_ref)


HEIGHT = 512


def specs(owners, count, rows, group):
    virt = owners * rows
    return dict(
        panel=pl.BlockSpec((HEIGHT, virt), lambda i: (i, 0)),
        amps=pl.BlockSpec((owners, count, rows, LANES), lambda i: (0, group, 0, 0)),
        half=pl.BlockSpec((owners, count, rows, LANES), lambda i: (0, 0, 0, 0)),
        part=pl.BlockSpec((count // 2, HEIGHT, 2 * LANES), lambda i: (0, i, 0)),
        base=pl.BlockSpec((HEIGHT, LANES), lambda i: (i, 0)),
        screen=pl.BlockSpec((count, HEIGHT // TILE, LANES), lambda i: (group, i, 0)),
        out=pl.BlockSpec((count, HEIGHT, LANES), lambda i: (group, i, 0)),
        energy=pl.BlockSpec(memory_space=pltpu.SMEM),
        wide=pltpu.VMEM((count // 2, virt, 2 * LANES), jnp.bfloat16),
    )


def cost(products, count, virt):
    return pl.CostEstimate(
        flops=2 * products * count * virt * virt * LANES,
        bytes_accessed=products * virt * virt * 2 + count * virt * LANES * 6,
        transcendentals=0,
    )


def update_whole(pair_energy, cycle, ladder, amps, half, base, screen, first):
    owners, count, rows, _ = half.shape
    virt = owners * rows
    at = specs(owners, count, rows, first // count)
    return pl.pallas_call(
        functools.partial(whole_kernel, first),
        grid=(virt // HEIGHT,),
        in_specs=[at[k] for k in ("energy", "panel", "panel", "amps", "half", "base", "screen")],
        out_specs=at["out"],
        out_shape=jax.ShapeDtypeStruct((amps.shape[1], virt, LANES), jnp.bfloat16),
        scratch_shapes=[at["wide"]] * 2,
        compiler_params=params(28),
        cost_estimate=cost(2, count, virt),
        name="update_whole",
    )(pair_energy, cycle, ladder, amps, half, base, screen)


def cycle_part(cycle, amps, first, count):
    owners, _, rows, _ = amps.shape
    virt = owners * rows
    at = specs(owners, count, rows, first // count)
    return pl.pallas_call(
        cycle_kernel,
        grid=(virt // HEIGHT,),
        in_specs=[at["panel"], at["amps"]],
        out_specs=at["part"],
        out_shape=jax.ShapeDtypeStruct((count // 2, virt, 2 * LANES), jnp.float32),
        scratch_shapes=[at["wide"]],
        compiler_params=params(20),
        cost_estimate=cost(1, count, virt),
        name="cycle_part",
    )(cycle, amps)


def update_ladder(pair_energy, ladder, half, part, base, screen, previous, first):
    owners, count, rows, _ = half.shape
    virt = owners * rows
    at = specs(owners, count, rows, first // count)
    return pl.pallas_call(
        functools.partial(ladder_kernel, first),
        grid=(virt // HEIGHT,),
        in_specs=[at[k] for k in ("energy", "panel", "half", "part", "base", "screen")]
        + [pl.BlockSpec(memory_space=pl.ANY)],
        out_specs=at["out"],
        out_shape=jax.ShapeDtypeStruct(previous.shape, previous.dtype),
        scratch_shapes=[at["wide"]],
        input_output_aliases={6: 0},
        compiler_params=params(24),
        cost_estimate=cost(1, count, virt),
        name="update_ladder",
    )(pair_energy, ladder, half, part, base, screen, previous)


def local(amplitudes, cycle_panel, ladder_panel, virt_energy, pair_energy, tile_mask):
    pairs = amplitudes.shape[0]
    count = pairs // CHUNKS
    exchange = functools.partial(
        lax.all_to_all, axis_name="virt", split_axis=0, concat_axis=0, tiled=True
    )
    gather = functools.partial(lax.all_gather, axis_name="pair", axis=0, tiled=True)
    after = lax.optimization_barrier
    with jax.named_scope("spread_panels"):
        rows, columns = ladder_panel.shape
        owners = columns // LANES
        both = jnp.concatenate([ladder_panel, cycle_panel])
        both = exchange(jnp.broadcast_to(both[None], (owners, 2 * rows, columns)))
        ladder_plane = both[:, :rows].reshape(owners * rows, columns)
        cycle_plane = both[:, rows:].reshape(owners * rows, columns)
    with jax.named_scope("gather_ladder"):
        ladder = gather(ladder_plane)
    with jax.named_scope("exchange_amplitudes"):
        own, _ = after((amplitudes, ladder_plane))
        amps = exchange(split_columns(own))
        own, cycle_plane, amps = after((own, cycle_plane, amps))
    with jax.named_scope("gather_cycle"):
        cycle = gather(cycle_plane)
    halves = []
    for chunk in range(CHUNKS):
        with jax.named_scope("half_ladder"):
            halves.append(exchange(half_ladder(own, ladder, chunk * count, count)))
    with jax.named_scope("update"):
        virt_energy, tile_mask, _ = after((virt_energy, tile_mask, halves[0]))
        column_start = lax.axis_index("virt") * LANES
        column_energy = lax.dynamic_slice_in_dim(virt_energy, column_start, LANES)
        base = virt_energy[:, None] + column_energy[None, :]
        screen = jnp.repeat(tile_mask.astype(jnp.float32), TILE, axis=2)
        out = update_whole(pair_energy, cycle, ladder, amps, halves[0], base, screen, 0)
        part = cycle_part(cycle, amps, count, count)
        return update_ladder(pair_energy, ladder, halves[1], part, base, screen, out, count)


def solution(mesh):
    in_specs = (
        P("pair", "virt", None),
        P(("pair", "virt"), None),
        P(("pair", "virt"), None),
        P(),
        P("pair"),
        P("pair", None, "virt"),
    )
    out_specs = P("pair", None, "virt")
    return jax.shard_map(local, mesh=mesh, in_specs=in_specs, out_specs=out_specs, check_vma=False)
```

```python
import functools

import jax
import jax.numpy as jnp
from jax import lax
from jax.experimental import pallas as pl
from jax.experimental.pallas import tpu as pltpu
from jax.sharding import PartitionSpec as P

TILE = 64
LANES = 128
CHUNKS = 2
MIB = 1024 * 1024
SMALL = pl.CostEstimate(flops=1, bytes_accessed=1, transcendentals=0)


def params(mib):
    return pltpu.CompilerParams(vmem_limit_bytes=mib * MIB)


def z_shift(pairs, k):
    return [(p, (p + 2 * k) % pairs) for p in range(pairs)]


def other_core(pairs):
    return [(p, p ^ 1) for p in range(pairs)]


PLACES = [(0, 0), (0, 1), (1, 0), (3, 1), (1, 1), (3, 0), (2, 0), (2, 1)]


def chip_of(pair, back, chips):
    return lax.rem(lax.div(pair, 2) - back + chips, chips)


def owner_of(pair, back, side, chips):
    core = lax.rem(pair, 2)
    return 2 * chip_of(pair, back, chips) + (1 - core if side else core)


def fetch_parts(pair, refs, panel, sems, backs=(0, 1, 2, 3)):
    chips = panel.shape[0] // 2
    for side in range(2):
        for i, (back, half) in enumerate(PLACES):
            if back not in backs:
                continue
            part = refs[side * len(PLACES) + i]
            rows = part.shape[0]
            target = panel.at[owner_of(pair, back, side, chips), pl.ds(half * rows, rows)]
            pltpu.make_async_copy(part, target, sems.at[side * chips + back]).start()


def wait_block(pair, back, side, panel, sems):
    chips = panel.shape[0] // 2
    block = panel.at[owner_of(pair, back, side, chips)]
    pltpu.make_async_copy(block, block, sems.at[side * chips + back]).wait()


def panel_shape(parts):
    rows, columns = parts[0].shape
    return (len(parts) // 2, 2 * rows, columns)


def split_kernel(a_ref, out_ref):
    pairs, rows, _ = a_ref.shape
    for v in range(out_ref.shape[0]):
        out_ref[v] = a_ref[:, :, v * LANES : (v + 1) * LANES].reshape(pairs * rows, LANES)


def split_columns(amplitudes):
    pairs, rows, columns = amplitudes.shape
    whole = pl.BlockSpec(memory_space=pltpu.VMEM)
    return pl.pallas_call(
        split_kernel,
        in_specs=[whole],
        out_specs=whole,
        out_shape=jax.ShapeDtypeStruct((columns // LANES, pairs * rows, LANES), amplitudes.dtype),
        compiler_params=params(8),
        cost_estimate=SMALL,
        name="split_columns",
    )(amplitudes)


def half_kernel(first, place_ref, a_ref, *refs):
    out_ref, left_ref, panel, left_done, sems = refs[-5:]
    ranks = panel.shape[0]
    width = out_ref.shape[0] // ranks
    fetch = pltpu.make_async_copy(a_ref.at[pl.ds(first, left_ref.shape[0])], left_ref, left_done)
    fetch.start()
    fetch_parts(place_ref[0], refs[:-5], panel, sems)
    fetch.wait()
    for side in range(2):
        for back in range(ranks // 2):
            wait_block(place_ref[0], back, side, panel, sems)
    left = left_ref[...].reshape(out_ref.shape[1], left_ref.shape[2])
    for rank in range(ranks):
        result = lax.dot_general(
            left, panel[rank], (((1,), (1,)), ((), ())), preferred_element_type=jnp.float32
        ).astype(jnp.bfloat16)
        for j in range(width):
            out_ref[rank * width + j] = result[:, j * LANES : (j + 1) * LANES]


def half_ladder(amplitudes, own, other, first, count):
    anywhere = pl.BlockSpec(memory_space=pl.ANY)
    _, rows, depth = amplitudes.shape
    parts = [*own, *other]
    shape = (depth // LANES, count * rows, LANES)
    return pl.pallas_call(
        functools.partial(half_kernel, first),
        grid=(1,),
        in_specs=[pl.BlockSpec(memory_space=pltpu.SMEM)] + [anywhere] * (1 + len(parts)),
        out_specs=pl.BlockSpec(shape, lambda i: (0, 0, 0)),
        out_shape=jax.ShapeDtypeStruct(shape, jnp.bfloat16),
        scratch_shapes=[
            pltpu.VMEM((count, rows, depth), jnp.bfloat16),
            pltpu.VMEM(panel_shape(parts), jnp.bfloat16),
            pltpu.SemaphoreType.DMA,
            pltpu.SemaphoreType.DMA((len(own),)),
        ],
        compiler_params=params(60),
        cost_estimate=pl.CostEstimate(
            flops=2 * count * rows * depth * depth, bytes_accessed=depth * depth * 2, transcendentals=0
        ),
        name="half_ladder",
    )(lax.axis_index("pair").reshape(1), amplitudes, *parts)


def widen(source, target):
    owners = source.shape[0]
    rows = target.shape[1] // owners
    for q in range(target.shape[0]):
        for side in range(2):
            r = 2 * q + side
            target[q, :, side * LANES : (side + 1) * LANES] = source[
                :, r * rows : (r + 1) * rows, :
            ].reshape(owners * rows, LANES)


def finish(first, total, q, energy_ref, base_ref, screen_ref, out_ref):
    height = total.shape[0]
    for side in range(2):
        r = 2 * q + side
        screen = jnp.broadcast_to(
            screen_ref[r][:, None, :], (height // TILE, TILE, LANES)
        ).reshape(height, LANES)
        masked = total[:, side * LANES : (side + 1) * LANES] * screen
        out_ref[r] = (masked / (base_ref[...] - energy_ref[first + r])).astype(out_ref.dtype)


BACKS = (0, 1, 3, 2)


def back_of(step):
    return jnp.where(step == 2, 3, jnp.where(step == 3, 2, step))


def main_kernel(place_ref, energy_ref, a_ref, h_ref, base_ref, screen_ref, *refs):
    parts = len(PLACES) * 2
    k_parts, l_parts = refs[:parts], refs[parts : 2 * parts]
    out_ref, next_ref, ladder_ref, k_panel, l_panel, a_wide, h_wide, k_sems, l_sems, store_sems = refs[
        2 * parts :
    ]
    i = pl.program_id(0)
    pair = place_ref[0]
    chips = len(BACKS)

    @pl.when(i == 0)
    def _():
        for back in BACKS:
            fetch_parts(pair, k_parts, k_panel, k_sems, (back,))
            fetch_parts(pair, l_parts, l_panel, l_sems, (back,))
        widen(a_ref, a_wide)
        widen(h_ref, h_wide)

    def store(owner):
        return pltpu.make_async_copy(l_panel.at[owner], ladder_ref.at[owner], store_sems.at[owner])

    back = back_of(i)
    for side in range(2):
        wait_block(pair, back, side, k_panel, k_sems)
        wait_block(pair, back, side, l_panel, l_sems)
        store(owner_of(pair, back, side, chips)).start()
    rows = pl.ds(2 * chip_of(pair, back, chips), 2)
    k = k_panel[rows].reshape(HEIGHT, k_panel.shape[2])
    l = l_panel[rows].reshape(HEIGHT, l_panel.shape[2])
    ready = h_wide.shape[0]
    for q in range(a_wide.shape[0]):
        total = jnp.dot(k, a_wide[q], preferred_element_type=jnp.float32)
        if q < ready:
            total += jnp.dot(l, h_wide[q], preferred_element_type=jnp.float32)
            finish(0, total, q, energy_ref, base_ref, screen_ref, out_ref)
        else:
            next_ref[q - ready] = total

    @pl.when(i == pl.num_programs(0) - 1)
    def _():
        for owner in range(l_panel.shape[0]):
            store(owner).wait()


def ladder_kernel(first, energy_ref, l_ref, h_ref, part_ref, base_ref, screen_ref, previous_ref, out_ref, h_wide):
    del previous_ref

    @pl.when(pl.program_id(0) == 0)
    def _():
        widen(h_ref, h_wide)

    for q in range(h_wide.shape[0]):
        total = part_ref[q] + jnp.dot(l_ref[...], h_wide[q], preferred_element_type=jnp.float32)
        finish(first, total, q, energy_ref, base_ref, screen_ref, out_ref)


HEIGHT = 512


def update_main(pair_energy, cycle_parts, ladder_parts, amps, half, base, screen):
    owners, height, _ = amps.shape
    pairs = pair_energy.shape[0]
    rows = height // pairs
    virt = owners * rows
    count = half.shape[1] // rows
    wide = [pltpu.VMEM((n // 2, virt, 2 * LANES), jnp.bfloat16) for n in (pairs, count)]
    anywhere = pl.BlockSpec(memory_space=pl.ANY)
    panel = panel_shape(cycle_parts)
    chips = len(BACKS)

    def chip(i, place):
        return chip_of(place[0], back_of(i), chips)

    def once(block):
        return pl.BlockSpec(block.shape, lambda i, place: (0, 0, 0), pipeline_mode=pl.Buffered(1))

    grid_spec = pltpu.PrefetchScalarGridSpec(
        num_scalar_prefetch=1,
        grid=(chips,),
        in_specs=[
            pl.BlockSpec(memory_space=pltpu.SMEM),
            once(amps),
            once(half),
            pl.BlockSpec((HEIGHT, LANES), lambda i, place: (chip(i, place), 0)),
            pl.BlockSpec((count, HEIGHT // TILE, LANES), lambda i, place: (0, chip(i, place), 0)),
        ]
        + [anywhere] * (len(cycle_parts) + len(ladder_parts)),
        out_specs=[
            pl.BlockSpec((count, HEIGHT, LANES), lambda i, place: (0, chip(i, place), 0)),
            pl.BlockSpec(
                ((pairs - count) // 2, HEIGHT, 2 * LANES), lambda i, place: (0, chip(i, place), 0)
            ),
            anywhere,
        ],
        scratch_shapes=[
            pltpu.VMEM(panel, jnp.bfloat16),
            pltpu.VMEM(panel, jnp.bfloat16),
            *wide,
        ]
        + [pltpu.SemaphoreType.DMA((panel[0],))] * 3,
    )
    return pl.pallas_call(
        main_kernel,
        grid_spec=grid_spec,
        out_shape=[
            jax.ShapeDtypeStruct((pairs, virt, LANES), jnp.bfloat16),
            jax.ShapeDtypeStruct(((pairs - count) // 2, virt, 2 * LANES), jnp.float32),
            jax.ShapeDtypeStruct(panel, jnp.bfloat16),
        ],
        compiler_params=params(60),
        cost_estimate=SMALL,
        name="update_main",
    )(
        lax.axis_index("pair").reshape(1), pair_energy, amps, half, base, screen,
        *cycle_parts, *ladder_parts,
    )


def update_ladder(pair_energy, ladder, half, part, base, screen, previous, first):
    owners = half.shape[0]
    virt = ladder.shape[0]
    count = half.shape[1] // (virt // owners)
    group = first // count
    height = HEIGHT
    return pl.pallas_call(
        functools.partial(ladder_kernel, first),
        grid=(virt // height,),
        in_specs=[
            pl.BlockSpec(memory_space=pltpu.SMEM),
            pl.BlockSpec((height, virt), lambda i: (i, 0)),
            pl.BlockSpec(half.shape, lambda i: (0, 0, 0)),
            pl.BlockSpec((count // 2, height, 2 * LANES), lambda i: (0, i, 0)),
            pl.BlockSpec((height, LANES), lambda i: (i, 0)),
            pl.BlockSpec((count, height // TILE, LANES), lambda i: (group, i, 0)),
            pl.BlockSpec(memory_space=pl.ANY),
        ],
        out_specs=pl.BlockSpec((count, height, LANES), lambda i: (group, i, 0)),
        out_shape=jax.ShapeDtypeStruct(previous.shape, previous.dtype),
        scratch_shapes=[pltpu.VMEM((count // 2, virt, 2 * LANES), jnp.bfloat16)],
        input_output_aliases={6: 0},
        compiler_params=params(60),
        cost_estimate=SMALL,
        name="update_ladder",
    )(pair_energy, ladder, half, part, base, screen, previous)


def local(amplitudes, cycle_panel, ladder_panel, virt_energy, pair_energy, tile_mask):
    pairs = amplitudes.shape[0]
    count = pairs // CHUNKS
    exchange = functools.partial(
        lax.all_to_all, axis_name="virt", split_axis=0, concat_axis=0, tiled=True
    )
    after = lax.optimization_barrier
    v = lax.axis_index("virt")
    rows, columns = ladder_panel.shape
    owners = columns // LANES
    ranks = virt_energy.shape[0] // (owners * rows)

    def along(part, step):
        return lax.ppermute(part, "pair", z_shift(ranks, step))

    def across(parts):
        return [lax.ppermute(part, "pair", other_core(ranks)) for part in parts]

    def first_parts(top, bottom):
        return [along(top, 1), along(bottom, 3)]

    def last_parts(top, bottom, first):
        return [along(bottom, 1), along(top, 3), along(first[0], 1), along(first[1], 3)]

    with jax.named_scope("spread_panels"):
        both = jnp.concatenate([ladder_panel, cycle_panel])
        both = exchange(jnp.broadcast_to(both[None], (owners, 2 * rows, columns)))
        middle = owners // 2
        halves = [
            both[i * middle : (i + 1) * middle, j * rows : (j + 1) * rows].reshape(-1, columns)
            for j in range(2)
            for i in range(2)
        ]
        halves, own = after((halves, amplitudes))
        ladder_halves, cycle_halves = halves[:2], halves[2:]
    with jax.named_scope("exchange_amplitudes"):
        amps = exchange(split_columns(own))
    with jax.named_scope("update"):
        virt_energy, tile_mask, _ = after((virt_energy, tile_mask, halves))
        column_energy = lax.dynamic_slice_in_dim(virt_energy, v * LANES, LANES)
        base = virt_energy[:, None] + column_energy[None, :]
        screen = jnp.repeat(tile_mask.astype(jnp.float32), TILE, axis=2)
    with jax.named_scope("gather_ladder"):
        first = first_parts(*ladder_halves)
        other = across(ladder_halves)
        first, other = after((first, other))
        last = last_parts(*ladder_halves, first)
        other += across(first)
        last, cycle_halves = after((last, cycle_halves))
        mine, other = ladder_halves + first + last, other + across(last)
    with jax.named_scope("gather_cycle"):
        first = first_parts(*cycle_halves)
    with jax.named_scope("half_ladder"):
        sent = half_ladder(amplitudes, mine, other, 0, count)
        sent, first, own, amps, base, screen = after((sent, first, amplitudes, amps, base, screen))
        half = exchange(sent)
    with jax.named_scope("gather_cycle"):
        last = last_parts(*cycle_halves, first)
        close = across(cycle_halves + first)
    with jax.named_scope("half_ladder"):
        sent = half_ladder(own, mine, other, count, count)
        last, sent = after((last, sent))
        half_tail = exchange(sent)
    with jax.named_scope("gather_cycle"):
        cycle_parts = cycle_halves + first + last + close + across(last)
    with jax.named_scope("update"):
        out, part, ladder = update_main(
            pair_energy, cycle_parts, mine + other, amps, half, base, screen
        )
        ladder = ladder.reshape(-1, columns)
        return update_ladder(pair_energy, ladder, half_tail, part, base, screen, out, count)


def solution(mesh):
    in_specs = (
        P("pair", "virt", None),
        P(("pair", "virt"), None),
        P(("pair", "virt"), None),
        P(),
        P("pair"),
        P("pair", None, "virt"),
    )
    out_specs = P("pair", None, "virt")
    return jax.shard_map(local, mesh=mesh, in_specs=in_specs, out_specs=out_specs, check_vma=False)
```

```python
import functools

import jax
import jax.numpy as jnp
from jax import lax
from jax.experimental import pallas as pl
from jax.experimental.pallas import tpu as pltpu
from jax.sharding import PartitionSpec as P

TILE = 64
LANES = 128
CHUNKS = 2
MIB = 1024 * 1024
SMALL = pl.CostEstimate(flops=1, bytes_accessed=1, transcendentals=0)


def params(mib):
    return pltpu.CompilerParams(vmem_limit_bytes=mib * MIB)


def z_shift(pairs, k):
    return [(p, (p + 2 * k) % pairs) for p in range(pairs)]


def other_core(pairs):
    return [(p, p ^ 1) for p in range(pairs)]


PLACES = [(0, 0), (0, 1), (1, 0), (3, 1), (1, 1), (3, 0), (2, 0), (2, 1)]


def chip_of(pair, back, chips):
    return lax.rem(lax.div(pair, 2) - back + chips, chips)


def owner_of(pair, back, side, chips):
    core = lax.rem(pair, 2)
    return 2 * chip_of(pair, back, chips) + (1 - core if side else core)


def fetch_parts(pair, refs, panel, sems, backs=(0, 1, 2, 3)):
    chips = panel.shape[0] // 2
    for side in range(2):
        for i, (back, half) in enumerate(PLACES):
            if back not in backs:
                continue
            part = refs[side * len(PLACES) + i]
            rows = part.shape[0]
            target = panel.at[owner_of(pair, back, side, chips), pl.ds(half * rows, rows)]
            pltpu.make_async_copy(part, target, sems.at[side * chips + back]).start()


def wait_block(pair, back, side, panel, sems):
    chips = panel.shape[0] // 2
    block = panel.at[owner_of(pair, back, side, chips)]
    pltpu.make_async_copy(block, block, sems.at[side * chips + back]).wait()


def panel_shape(parts):
    rows, columns = parts[0].shape
    return (len(parts) // 2, 2 * rows, columns)


def split_kernel(a_ref, out_ref, sems):
    copies = [
        pltpu.make_async_copy(a_ref.at[:, :, pl.ds(v * LANES, LANES)], out_ref.at[v], sems.at[v])
        for v in range(out_ref.shape[0])
    ]
    for copy in copies:
        copy.start()
    for copy in copies:
        copy.wait()


def split_columns(amplitudes):
    pairs, rows, columns = amplitudes.shape
    owners = columns // LANES
    blocks = pl.pallas_call(
        split_kernel,
        in_specs=[pl.BlockSpec(memory_space=pltpu.VMEM)],
        out_specs=pl.BlockSpec(memory_space=pl.ANY),
        out_shape=pltpu.HBM((owners, pairs, rows, LANES), amplitudes.dtype),
        scratch_shapes=[pltpu.SemaphoreType.DMA((owners,))],
        compiler_params=params(8),
        cost_estimate=SMALL,
        name="split_columns",
    )(amplitudes)
    return blocks.reshape(owners, pairs * rows, LANES)


def half_kernel(first, place_ref, a_ref, *refs):
    out_ref, left_ref, panel, left_done, sems = refs[-5:]
    ranks = panel.shape[0]
    width = out_ref.shape[0] // ranks
    fetch = pltpu.make_async_copy(a_ref.at[pl.ds(first, left_ref.shape[0])], left_ref, left_done)
    fetch.start()
    fetch_parts(place_ref[0], refs[:-5], panel, sems)
    fetch.wait()
    for side in range(2):
        for back in range(ranks // 2):
            wait_block(place_ref[0], back, side, panel, sems)
    left = left_ref[...].reshape(out_ref.shape[1], left_ref.shape[2])
    for rank in range(ranks):
        result = lax.dot_general(
            left, panel[rank], (((1,), (1,)), ((), ())), preferred_element_type=jnp.float32
        ).astype(jnp.bfloat16)
        for j in range(width):
            out_ref[rank * width + j] = result[:, j * LANES : (j + 1) * LANES]


def half_ladder(amplitudes, own, other, first, count):
    anywhere = pl.BlockSpec(memory_space=pl.ANY)
    _, rows, depth = amplitudes.shape
    parts = [*own, *other]
    shape = (depth // LANES, count * rows, LANES)
    return pl.pallas_call(
        functools.partial(half_kernel, first),
        grid=(1,),
        in_specs=[pl.BlockSpec(memory_space=pltpu.SMEM)] + [anywhere] * (1 + len(parts)),
        out_specs=pl.BlockSpec(shape, lambda i: (0, 0, 0)),
        out_shape=jax.ShapeDtypeStruct(shape, jnp.bfloat16),
        scratch_shapes=[
            pltpu.VMEM((count, rows, depth), jnp.bfloat16),
            pltpu.VMEM(panel_shape(parts), jnp.bfloat16),
            pltpu.SemaphoreType.DMA,
            pltpu.SemaphoreType.DMA((len(own),)),
        ],
        compiler_params=params(60),
        cost_estimate=pl.CostEstimate(
            flops=2 * count * rows * depth * depth, bytes_accessed=depth * depth * 2, transcendentals=0
        ),
        name="half_ladder",
    )(lax.axis_index("pair").reshape(1), amplitudes, *parts)


def widen(source, target):
    owners = source.shape[0]
    rows = target.shape[1] // owners
    for q in range(target.shape[0]):
        for side in range(2):
            r = 2 * q + side
            target[q, :, side * LANES : (side + 1) * LANES] = source[
                :, r * rows : (r + 1) * rows, :
            ].reshape(owners * rows, LANES)


def finish(first, total, q, energy_ref, base_ref, screen_ref, out_ref):
    height = total.shape[0]
    for side in range(2):
        r = 2 * q + side
        screen = jnp.broadcast_to(
            screen_ref[r][:, None, :], (height // TILE, TILE, LANES)
        ).reshape(height, LANES)
        masked = total[:, side * LANES : (side + 1) * LANES] * screen
        out_ref[r] = (masked / (base_ref[...] - energy_ref[first + r])).astype(out_ref.dtype)


BACKS = (0, 1, 3, 2)


def back_of(step):
    return jnp.where(step == 2, 3, jnp.where(step == 3, 2, step))


def main_kernel(place_ref, energy_ref, a_ref, h_ref, base_ref, screen_ref, *refs):
    parts = len(PLACES) * 2
    k_parts, l_parts = refs[:parts], refs[parts : 2 * parts]
    out_ref, next_ref, ladder_ref, k_panel, l_panel, a_wide, h_wide, k_sems, l_sems, store_sems = refs[
        2 * parts :
    ]
    i = pl.program_id(0)
    pair = place_ref[0]
    chips = len(BACKS)

    @pl.when(i == 0)
    def _():
        for back in BACKS:
            fetch_parts(pair, k_parts, k_panel, k_sems, (back,))
            fetch_parts(pair, l_parts, l_panel, l_sems, (back,))
        widen(a_ref, a_wide)
        widen(h_ref, h_wide)

    def store(owner):
        return pltpu.make_async_copy(l_panel.at[owner], ladder_ref.at[owner], store_sems.at[owner])

    back = back_of(i)
    for side in range(2):
        wait_block(pair, back, side, k_panel, k_sems)
        wait_block(pair, back, side, l_panel, l_sems)
        store(owner_of(pair, back, side, chips)).start()
    rows = pl.ds(2 * chip_of(pair, back, chips), 2)
    k = k_panel[rows].reshape(HEIGHT, k_panel.shape[2])
    l = l_panel[rows].reshape(HEIGHT, l_panel.shape[2])
    ready = h_wide.shape[0]
    for q in range(a_wide.shape[0]):
        total = jnp.dot(k, a_wide[q], preferred_element_type=jnp.float32)
        if q < ready:
            total += jnp.dot(l, h_wide[q], preferred_element_type=jnp.float32)
            finish(0, total, q, energy_ref, base_ref, screen_ref, out_ref)
        else:
            next_ref[q - ready] = total

    @pl.when(i == pl.num_programs(0) - 1)
    def _():
        for owner in range(l_panel.shape[0]):
            store(owner).wait()


def ladder_kernel(first, energy_ref, l_ref, h_ref, part_ref, base_ref, screen_ref, previous_ref, out_ref, h_wide):
    del previous_ref

    @pl.when(pl.program_id(0) == 0)
    def _():
        widen(h_ref, h_wide)

    for q in range(h_wide.shape[0]):
        total = part_ref[q] + jnp.dot(l_ref[...], h_wide[q], preferred_element_type=jnp.float32)
        finish(first, total, q, energy_ref, base_ref, screen_ref, out_ref)


HEIGHT = 512


def keep_in(space, values):
    return [pltpu.with_memory_space_constraint(value, space) for value in values]


def update_main(pair_energy, cycle_parts, ladder_parts, amps, half, base, screen):
    owners, height, _ = amps.shape
    pairs = pair_energy.shape[0]
    rows = height // pairs
    virt = owners * rows
    count = half.shape[1] // rows
    wide = [pltpu.VMEM((n // 2, virt, 2 * LANES), jnp.bfloat16) for n in (pairs, count)]
    anywhere = pl.BlockSpec(memory_space=pl.ANY)
    panel = panel_shape(cycle_parts)
    chips = len(BACKS)

    def chip(i, place):
        return chip_of(place[0], back_of(i), chips)

    def once(block):
        return pl.BlockSpec(block.shape, lambda i, place: (0, 0, 0), pipeline_mode=pl.Buffered(1))

    grid_spec = pltpu.PrefetchScalarGridSpec(
        num_scalar_prefetch=1,
        grid=(chips,),
        in_specs=[
            pl.BlockSpec(memory_space=pltpu.SMEM),
            once(amps),
            once(half),
            pl.BlockSpec((HEIGHT, LANES), lambda i, place: (chip(i, place), 0)),
            pl.BlockSpec((count, HEIGHT // TILE, LANES), lambda i, place: (0, chip(i, place), 0)),
        ]
        + [anywhere] * (len(cycle_parts) + len(ladder_parts)),
        out_specs=[
            pl.BlockSpec((count, HEIGHT, LANES), lambda i, place: (0, chip(i, place), 0)),
            pl.BlockSpec(
                ((pairs - count) // 2, HEIGHT, 2 * LANES), lambda i, place: (0, chip(i, place), 0)
            ),
            anywhere,
        ],
        scratch_shapes=[
            pltpu.VMEM(panel, jnp.bfloat16),
            pltpu.VMEM(panel, jnp.bfloat16),
            *wide,
        ]
        + [pltpu.SemaphoreType.DMA((panel[0],))] * 3,
    )
    return pl.pallas_call(
        main_kernel,
        grid_spec=grid_spec,
        out_shape=[
            jax.ShapeDtypeStruct((pairs, virt, LANES), jnp.bfloat16),
            pltpu.HBM(((pairs - count) // 2, virt, 2 * LANES), jnp.float32),
            pltpu.HBM(panel, jnp.bfloat16),
        ],
        compiler_params=params(40),
        cost_estimate=SMALL,
        name="update_main",
    )(
        lax.axis_index("pair").reshape(1), pair_energy, amps, half, base, screen,
        *keep_in(pltpu.HBM, cycle_parts), *keep_in(pltpu.HBM, ladder_parts),
    )


def update_ladder(pair_energy, ladder, half, part, base, screen, previous, first):
    owners = half.shape[0]
    virt = ladder.shape[0]
    count = half.shape[1] // (virt // owners)
    group = first // count
    height = HEIGHT
    return pl.pallas_call(
        functools.partial(ladder_kernel, first),
        grid=(virt // height,),
        in_specs=[
            pl.BlockSpec(memory_space=pltpu.SMEM),
            pl.BlockSpec((height, virt), lambda i: (i, 0)),
            pl.BlockSpec(memory_space=pltpu.VMEM),
            pl.BlockSpec((count // 2, height, 2 * LANES), lambda i: (0, i, 0)),
            pl.BlockSpec((height, LANES), lambda i: (i, 0)),
            pl.BlockSpec((count, height // TILE, LANES), lambda i: (group, i, 0)),
            pl.BlockSpec(memory_space=pl.ANY),
        ],
        out_specs=pl.BlockSpec((count, height, LANES), lambda i: (group, i, 0)),
        out_shape=jax.ShapeDtypeStruct(previous.shape, previous.dtype),
        scratch_shapes=[pltpu.VMEM((count // 2, virt, 2 * LANES), jnp.bfloat16)],
        input_output_aliases={6: 0},
        compiler_params=params(24),
        cost_estimate=SMALL,
        name="update_ladder",
    )(pair_energy, *keep_in(pltpu.HBM, [ladder]), half, *keep_in(pltpu.HBM, [part]), base, screen, previous)


def local(amplitudes, cycle_panel, ladder_panel, virt_energy, pair_energy, tile_mask):
    pairs = amplitudes.shape[0]
    count = pairs // CHUNKS
    exchange = functools.partial(
        lax.all_to_all, axis_name="virt", split_axis=0, concat_axis=0, tiled=True
    )
    after = lax.optimization_barrier
    v = lax.axis_index("virt")
    rows, columns = ladder_panel.shape
    owners = columns // LANES
    ranks = virt_energy.shape[0] // (owners * rows)

    def along(part, step):
        return lax.ppermute(part, "pair", z_shift(ranks, step))

    def across(parts):
        return [lax.ppermute(part, "pair", other_core(ranks)) for part in parts]

    def first_parts(top, bottom):
        return [along(top, 1), along(bottom, 3)]

    def last_parts(top, bottom, first):
        return [along(bottom, 1), along(top, 3), along(first[0], 1), along(first[1], 3)]

    with jax.named_scope("spread_panels"):
        both = jnp.concatenate([ladder_panel, cycle_panel])
        both = exchange(jnp.broadcast_to(both[None], (owners, 2 * rows, columns)))
        middle = owners // 2
        halves = [
            both[i * middle : (i + 1) * middle, j * rows : (j + 1) * rows].reshape(-1, columns)
            for j in range(2)
            for i in range(2)
        ]
        halves, own = after((halves, amplitudes))
        ladder_halves, cycle_halves = halves[:2], halves[2:]
    with jax.named_scope("exchange_amplitudes"):
        amps = exchange(split_columns(own))
    with jax.named_scope("update"):
        virt_energy, tile_mask, _ = after((virt_energy, tile_mask, halves))
        column_energy = lax.dynamic_slice_in_dim(virt_energy, v * LANES, LANES)
        base = virt_energy[:, None] + column_energy[None, :]
        screen = jnp.repeat(tile_mask.astype(jnp.float32), TILE, axis=2)
    with jax.named_scope("gather_ladder"):
        first = first_parts(*ladder_halves)
        other = across(ladder_halves)
        first, other = after((first, other))
        last = last_parts(*ladder_halves, first)
        other += across(first)
        last, cycle_halves = after((last, cycle_halves))
        mine, other = ladder_halves + first + last, other + across(last)
    with jax.named_scope("gather_cycle"):
        first = first_parts(*cycle_halves)
    with jax.named_scope("half_ladder"):
        sent = half_ladder(amplitudes, mine, other, 0, count)
        sent, first, own, amps, base, screen = after((sent, first, amplitudes, amps, base, screen))
        half = exchange(sent)
    with jax.named_scope("gather_cycle"):
        last = last_parts(*cycle_halves, first)
        close = across(cycle_halves + first)
    with jax.named_scope("half_ladder"):
        sent = half_ladder(own, mine, other, count, count)
        last, sent = after((last, sent))
        half_tail = exchange(sent)
    with jax.named_scope("gather_cycle"):
        cycle_parts = cycle_halves + first + last + close + across(last)
    with jax.named_scope("update"):
        out, part, ladder = update_main(
            pair_energy, cycle_parts, mine + other, amps, half, base, screen
        )
        ladder = ladder.reshape(-1, columns)
        return update_ladder(pair_energy, ladder, half_tail, part, base, screen, out, count)


def solution(mesh):
    in_specs = (
        P("pair", "virt", None),
        P(("pair", "virt"), None),
        P(("pair", "virt"), None),
        P(),
        P("pair"),
        P("pair", None, "virt"),
    )
    out_specs = P("pair", None, "virt")
    return jax.shard_map(local, mesh=mesh, in_specs=in_specs, out_specs=out_specs, check_vma=False)
```

```python
import functools

import jax
import jax.numpy as jnp
from jax import lax
from jax.experimental import pallas as pl
from jax.experimental.pallas import tpu as pltpu
from jax.sharding import PartitionSpec as P

TILE = 64
LANES = 128
CHUNKS = 2
MIB = 1024 * 1024
SMALL = pl.CostEstimate(flops=1, bytes_accessed=1, transcendentals=0)


def params(mib):
    return pltpu.CompilerParams(vmem_limit_bytes=mib * MIB)


def z_shift(pairs, k):
    return [(p, (p + 2 * k) % pairs) for p in range(pairs)]


def other_core(pairs):
    return [(p, p ^ 1) for p in range(pairs)]


PLACES = [(0, 0), (0, 1), (1, 0), (3, 1), (1, 1), (3, 0), (2, 0), (2, 1)]


def chip_of(pair, back, chips):
    return lax.rem(lax.div(pair, 2) - back + chips, chips)


def owner_of(pair, back, side, chips):
    core = lax.rem(pair, 2)
    return 2 * chip_of(pair, back, chips) + (1 - core if side else core)


def fetch_parts(pair, refs, panel, sems, backs=(0, 1, 2, 3)):
    chips = panel.shape[0] // 2
    for side in range(2):
        for i, (back, half) in enumerate(PLACES):
            if back not in backs:
                continue
            part = refs[side * len(PLACES) + i]
            rows = part.shape[0]
            target = panel.at[owner_of(pair, back, side, chips), pl.ds(half * rows, rows)]
            pltpu.make_async_copy(part, target, sems.at[side * chips + back]).start()


def wait_block(pair, back, side, panel, sems):
    chips = panel.shape[0] // 2
    block = panel.at[owner_of(pair, back, side, chips)]
    pltpu.make_async_copy(block, block, sems.at[side * chips + back]).wait()


def panel_shape(parts):
    rows, columns = parts[0].shape
    return (len(parts) // 2, 2 * rows, columns)


def split_kernel(a_ref, out_ref, sems):
    copies = [
        pltpu.make_async_copy(a_ref.at[:, :, pl.ds(v * LANES, LANES)], out_ref.at[v], sems.at[v])
        for v in range(out_ref.shape[0])
    ]
    for copy in copies:
        copy.start()
    for copy in copies:
        copy.wait()


def split_columns(amplitudes):
    pairs, rows, columns = amplitudes.shape
    owners = columns // LANES
    blocks = pl.pallas_call(
        split_kernel,
        in_specs=[pl.BlockSpec(memory_space=pltpu.VMEM)],
        out_specs=pl.BlockSpec(memory_space=pl.ANY),
        out_shape=pltpu.HBM((owners, pairs, rows, LANES), amplitudes.dtype),
        scratch_shapes=[pltpu.SemaphoreType.DMA((owners,))],
        compiler_params=params(8),
        cost_estimate=SMALL,
        name="split_columns",
    )(amplitudes)
    return blocks.reshape(owners, pairs * rows, LANES)


def half_kernel(first, place_ref, a_ref, *refs):
    out_ref, left_ref, panel, left_done, sems = refs[-5:]
    ranks = panel.shape[0]
    width = out_ref.shape[0] // ranks
    fetch = pltpu.make_async_copy(a_ref.at[pl.ds(first, left_ref.shape[0])], left_ref, left_done)
    fetch.start()
    fetch_parts(place_ref[0], refs[:-5], panel, sems)
    fetch.wait()
    for side in range(2):
        for back in range(ranks // 2):
            wait_block(place_ref[0], back, side, panel, sems)
    left = left_ref[...].reshape(out_ref.shape[1], left_ref.shape[2])
    for rank in range(ranks):
        result = lax.dot_general(
            left, panel[rank], (((1,), (1,)), ((), ())), preferred_element_type=jnp.float32
        ).astype(jnp.bfloat16)
        for j in range(width):
            out_ref[rank * width + j] = result[:, j * LANES : (j + 1) * LANES]


def half_ladder(amplitudes, own, other, first, count):
    anywhere = pl.BlockSpec(memory_space=pl.ANY)
    _, rows, depth = amplitudes.shape
    parts = [*own, *other]
    shape = (depth // LANES, count * rows, LANES)
    return pl.pallas_call(
        functools.partial(half_kernel, first),
        grid=(1,),
        in_specs=[pl.BlockSpec(memory_space=pltpu.SMEM)] + [anywhere] * (1 + len(parts)),
        out_specs=pl.BlockSpec(shape, lambda i: (0, 0, 0)),
        out_shape=jax.ShapeDtypeStruct(shape, jnp.bfloat16),
        scratch_shapes=[
            pltpu.VMEM((count, rows, depth), jnp.bfloat16),
            pltpu.VMEM(panel_shape(parts), jnp.bfloat16),
            pltpu.SemaphoreType.DMA,
            pltpu.SemaphoreType.DMA((len(own),)),
        ],
        compiler_params=params(60),
        cost_estimate=pl.CostEstimate(
            flops=2 * count * rows * depth * depth, bytes_accessed=depth * depth * 2, transcendentals=0
        ),
        name="half_ladder",
    )(lax.axis_index("pair").reshape(1), amplitudes, *parts)


def widen(source, target):
    owners = source.shape[0]
    rows = target.shape[1] // owners
    for q in range(target.shape[0]):
        for side in range(2):
            r = 2 * q + side
            target[q, :, side * LANES : (side + 1) * LANES] = source[
                :, r * rows : (r + 1) * rows, :
            ].reshape(owners * rows, LANES)


def finish(first, total, q, energy_ref, base_ref, screen_ref, out_ref):
    height = total.shape[0]
    for side in range(2):
        r = 2 * q + side
        screen = jnp.broadcast_to(
            screen_ref[r][:, None, :], (height // TILE, TILE, LANES)
        ).reshape(height, LANES)
        masked = total[:, side * LANES : (side + 1) * LANES] * screen
        out_ref[r] = (masked / (base_ref[...] - energy_ref[first + r])).astype(out_ref.dtype)


BACKS = (0, 1, 3, 2)


def back_of(step):
    return jnp.where(step == 2, 3, jnp.where(step == 3, 2, step))


def main_kernel(place_ref, energy_ref, a_ref, h_ref, base_ref, screen_ref, *refs):
    parts = len(PLACES) * 2
    k_parts, l_parts = refs[:parts], refs[parts : 2 * parts]
    out_ref, next_ref, ladder_ref, k_panel, l_panel, a_wide, h_wide, k_sems, l_sems, store_sems = refs[
        2 * parts :
    ]
    i = pl.program_id(0)
    pair = place_ref[0]
    chips = len(BACKS)

    @pl.when(i == 0)
    def _():
        for back in BACKS:
            fetch_parts(pair, k_parts, k_panel, k_sems, (back,))
            fetch_parts(pair, l_parts, l_panel, l_sems, (back,))
        widen(a_ref, a_wide)
        widen(h_ref, h_wide)

    def store(owner):
        return pltpu.make_async_copy(l_panel.at[owner], ladder_ref.at[owner], store_sems.at[owner])

    back = back_of(i)
    for side in range(2):
        wait_block(pair, back, side, k_panel, k_sems)
        wait_block(pair, back, side, l_panel, l_sems)
        store(owner_of(pair, back, side, chips)).start()
    rows = pl.ds(2 * chip_of(pair, back, chips), 2)
    k = k_panel[rows].reshape(HEIGHT, k_panel.shape[2])
    l = l_panel[rows].reshape(HEIGHT, l_panel.shape[2])
    ready = h_wide.shape[0]
    for q in range(a_wide.shape[0]):
        total = jnp.dot(k, a_wide[q], preferred_element_type=jnp.float32)
        if q < ready:
            total += jnp.dot(l, h_wide[q], preferred_element_type=jnp.float32)
            finish(0, total, q, energy_ref, base_ref, screen_ref, out_ref)
        else:
            next_ref[q - ready] = total

    @pl.when(i == pl.num_programs(0) - 1)
    def _():
        for owner in range(l_panel.shape[0]):
            store(owner).wait()


def ladder_kernel(
    first, cuts, energy_ref, l_hbm, h_ref, part_hbm, base_hbm, screen_ref, previous_ref, out_hbm,
    l_ref, part_ref, base_ref, out_ref, h_wide, sems, out_done,
):
    del previous_ref
    count = out_ref.shape[0]
    spans = [pl.ds(low, high - low) for low, high in zip(cuts, cuts[1:])]

    def loads(i):
        rows = spans[i]
        return [
            pltpu.make_async_copy(l_hbm.at[rows], l_ref.at[rows], sems.at[i, 0]),
            pltpu.make_async_copy(part_hbm.at[:, rows], part_ref.at[:, rows], sems.at[i, 1]),
            pltpu.make_async_copy(base_hbm.at[rows], base_ref.at[rows], sems.at[i, 2]),
        ]

    def store(i):
        rows = spans[i]
        return pltpu.make_async_copy(
            out_ref.at[:, rows], out_hbm.at[pl.ds(first, count), rows], out_done.at[i]
        )

    for i in range(2):
        for load in loads(i):
            load.start()
    widen(h_ref, h_wide)
    for i, rows in enumerate(spans):
        for load in loads(i):
            load.wait()
        if i + 2 < len(spans):
            for load in loads(i + 2):
                load.start()
        tiles = pl.ds(rows.start // TILE, rows.size // TILE)
        for q in range(h_wide.shape[0]):
            total = part_ref[q, rows] + jnp.dot(
                l_ref[rows], h_wide[q], preferred_element_type=jnp.float32
            )
            finish(
                first, total, q, energy_ref, base_ref.at[rows],
                screen_ref.at[pl.ds(first, count), tiles], out_ref.at[:, rows],
            )
        store(i).start()
    for i in range(len(spans)):
        store(i).wait()


HEIGHT = 512


def keep_in(space, values):
    return [pltpu.with_memory_space_constraint(value, space) for value in values]


def update_main(pair_energy, cycle_parts, ladder_parts, amps, half, base, screen):
    owners, height, _ = amps.shape
    pairs = pair_energy.shape[0]
    rows = height // pairs
    virt = owners * rows
    count = half.shape[1] // rows
    wide = [pltpu.VMEM((n // 2, virt, 2 * LANES), jnp.bfloat16) for n in (pairs, count)]
    anywhere = pl.BlockSpec(memory_space=pl.ANY)
    panel = panel_shape(cycle_parts)
    chips = len(BACKS)

    def chip(i, place):
        return chip_of(place[0], back_of(i), chips)

    def once(block):
        return pl.BlockSpec(block.shape, lambda i, place: (0, 0, 0), pipeline_mode=pl.Buffered(1))

    grid_spec = pltpu.PrefetchScalarGridSpec(
        num_scalar_prefetch=1,
        grid=(chips,),
        in_specs=[
            pl.BlockSpec(memory_space=pltpu.SMEM),
            once(amps),
            once(half),
            pl.BlockSpec((HEIGHT, LANES), lambda i, place: (chip(i, place), 0)),
            pl.BlockSpec((count, HEIGHT // TILE, LANES), lambda i, place: (0, chip(i, place), 0)),
        ]
        + [anywhere] * (len(cycle_parts) + len(ladder_parts)),
        out_specs=[
            pl.BlockSpec((count, HEIGHT, LANES), lambda i, place: (0, chip(i, place), 0)),
            pl.BlockSpec(
                ((pairs - count) // 2, HEIGHT, 2 * LANES), lambda i, place: (0, chip(i, place), 0)
            ),
            anywhere,
        ],
        scratch_shapes=[
            pltpu.VMEM(panel, jnp.bfloat16),
            pltpu.VMEM(panel, jnp.bfloat16),
            *wide,
        ]
        + [pltpu.SemaphoreType.DMA((panel[0],))] * 3,
    )
    return pl.pallas_call(
        main_kernel,
        grid_spec=grid_spec,
        out_shape=[
            jax.ShapeDtypeStruct((pairs, virt, LANES), jnp.bfloat16),
            pltpu.HBM(((pairs - count) // 2, virt, 2 * LANES), jnp.float32),
            pltpu.HBM(panel, jnp.bfloat16),
        ],
        compiler_params=params(40),
        cost_estimate=SMALL,
        name="update_main",
    )(
        lax.axis_index("pair").reshape(1), pair_energy, amps, half, base, screen,
        *keep_in(pltpu.HBM, cycle_parts), *keep_in(pltpu.HBM, ladder_parts),
    )


def update_ladder(pair_energy, ladder, half, part, base, screen, previous, first):
    owners = half.shape[0]
    virt = ladder.shape[0]
    count = half.shape[1] // (virt // owners)
    cuts = (0, HEIGHT // 2, *range(3 * HEIGHT // 2, virt, HEIGHT), virt)
    steps = len(cuts) - 1
    anywhere = pl.BlockSpec(memory_space=pl.ANY)
    whole = pl.BlockSpec(memory_space=pltpu.VMEM)
    return pl.pallas_call(
        functools.partial(ladder_kernel, first, cuts),
        in_specs=[
            pl.BlockSpec(memory_space=pltpu.SMEM),
            anywhere,
            whole,
            anywhere,
            anywhere,
            whole,
            anywhere,
        ],
        out_specs=anywhere,
        out_shape=jax.ShapeDtypeStruct(previous.shape, previous.dtype),
        scratch_shapes=[
            pltpu.VMEM(ladder.shape, jnp.bfloat16),
            pltpu.VMEM(part.shape, jnp.float32),
            pltpu.VMEM(base.shape, jnp.float32),
            pltpu.VMEM((count, virt, LANES), jnp.bfloat16),
            pltpu.VMEM((count // 2, virt, 2 * LANES), jnp.bfloat16),
            pltpu.SemaphoreType.DMA((steps, 3)),
            pltpu.SemaphoreType.DMA((steps,)),
        ],
        input_output_aliases={6: 0},
        compiler_params=params(28),
        cost_estimate=SMALL,
        name="update_ladder",
    )(
        pair_energy, *keep_in(pltpu.HBM, [ladder]), half, *keep_in(pltpu.HBM, [part]), base, screen,
        previous,
    )


def local(amplitudes, cycle_panel, ladder_panel, virt_energy, pair_energy, tile_mask):
    pairs = amplitudes.shape[0]
    count = pairs // CHUNKS
    exchange = functools.partial(
        lax.all_to_all, axis_name="virt", split_axis=0, concat_axis=0, tiled=True
    )
    after = lax.optimization_barrier
    v = lax.axis_index("virt")
    rows, columns = ladder_panel.shape
    owners = columns // LANES
    ranks = virt_energy.shape[0] // (owners * rows)

    def along(part, step):
        return lax.ppermute(part, "pair", z_shift(ranks, step))

    def across(parts):
        return [lax.ppermute(part, "pair", other_core(ranks)) for part in parts]

    def first_parts(top, bottom):
        return [along(top, 1), along(bottom, 3)]

    def last_parts(top, bottom, first):
        return [along(bottom, 1), along(top, 3), along(first[0], 1), along(first[1], 3)]

    with jax.named_scope("spread_panels"):
        both = jnp.concatenate([ladder_panel, cycle_panel])
        both = exchange(jnp.broadcast_to(both[None], (owners, 2 * rows, columns)))
        middle = owners // 2
        halves = [
            both[i * middle : (i + 1) * middle, j * rows : (j + 1) * rows].reshape(-1, columns)
            for j in range(2)
            for i in range(2)
        ]
        halves, own = after((halves, amplitudes))
        ladder_halves, cycle_halves = halves[:2], halves[2:]
    with jax.named_scope("exchange_amplitudes"):
        amps = exchange(split_columns(own))
    with jax.named_scope("update"):
        virt_energy, tile_mask, _ = after((virt_energy, tile_mask, halves))
        column_energy = lax.dynamic_slice_in_dim(virt_energy, v * LANES, LANES)
        base = virt_energy[:, None] + column_energy[None, :]
        screen = jnp.repeat(tile_mask.astype(jnp.float32), TILE, axis=2)
    with jax.named_scope("gather_ladder"):
        first = first_parts(*ladder_halves)
        other = across(ladder_halves)
        first, other = after((first, other))
        last = last_parts(*ladder_halves, first)
        other += across(first)
        last, cycle_halves = after((last, cycle_halves))
        mine, other = ladder_halves + first + last, other + across(last)
    with jax.named_scope("gather_cycle"):
        first = first_parts(*cycle_halves)
    with jax.named_scope("half_ladder"):
        sent = half_ladder(amplitudes, mine, other, 0, count)
        sent, first, own, amps, base, screen = after((sent, first, amplitudes, amps, base, screen))
        half = exchange(sent)
    with jax.named_scope("gather_cycle"):
        last = last_parts(*cycle_halves, first)
        close = across(cycle_halves + first)
    with jax.named_scope("half_ladder"):
        sent = half_ladder(own, mine, other, count, count)
        last, sent = after((last, sent))
        half_tail = exchange(sent)
    with jax.named_scope("gather_cycle"):
        cycle_parts = cycle_halves + first + last + close + across(last)
    with jax.named_scope("update"):
        out, part, ladder = update_main(
            pair_energy, cycle_parts, mine + other, amps, half, base, screen
        )
        ladder = ladder.reshape(-1, columns)
        return update_ladder(pair_energy, ladder, half_tail, part, base, screen, out, count)


def solution(mesh):
    in_specs = (
        P("pair", "virt", None),
        P(("pair", "virt"), None),
        P(("pair", "virt"), None),
        P(),
        P("pair"),
        P("pair", None, "virt"),
    )
    out_specs = P("pair", None, "virt")
    return jax.shard_map(local, mesh=mesh, in_specs=in_specs, out_specs=out_specs, check_vma=False)
```

```python
import functools

import jax
import jax.numpy as jnp
from jax import lax
from jax.experimental import pallas as pl
from jax.experimental.pallas import tpu as pltpu
from jax.sharding import PartitionSpec as P

TILE = 64
LANES = 128
CHUNKS = 2
MIB = 1024 * 1024
SMALL = pl.CostEstimate(flops=1, bytes_accessed=1, transcendentals=0)


def params(mib):
    return pltpu.CompilerParams(vmem_limit_bytes=mib * MIB)


def z_shift(pairs, k):
    return [(p, (p + 2 * k) % pairs) for p in range(pairs)]


def other_core(pairs):
    return [(p, p ^ 1) for p in range(pairs)]


PLACES = [(0, 0), (0, 1), (1, 0), (3, 1), (1, 1), (3, 0), (2, 0), (2, 1)]


def chip_of(pair, back, chips):
    return lax.rem(lax.div(pair, 2) - back + chips, chips)


def owner_of(pair, back, side, chips):
    core = lax.rem(pair, 2)
    return 2 * chip_of(pair, back, chips) + (1 - core if side else core)


def fetch_parts(pair, refs, panel, sems, backs=(0, 1, 2, 3)):
    chips = panel.shape[0] // 2
    for side in range(2):
        for i, (back, half) in enumerate(PLACES):
            if back not in backs:
                continue
            part = refs[side * len(PLACES) + i]
            rows = part.shape[0]
            target = panel.at[owner_of(pair, back, side, chips), pl.ds(half * rows, rows)]
            pltpu.make_async_copy(part, target, sems.at[side * chips + back]).start()


def wait_block(pair, back, side, panel, sems):
    chips = panel.shape[0] // 2
    block = panel.at[owner_of(pair, back, side, chips)]
    pltpu.make_async_copy(block, block, sems.at[side * chips + back]).wait()


def panel_shape(parts):
    rows, columns = parts[0].shape
    return (len(parts) // 2, 2 * rows, columns)


def split_kernel(a_ref, out_ref, sems):
    copies = [
        pltpu.make_async_copy(a_ref.at[:, :, pl.ds(v * LANES, LANES)], out_ref.at[v], sems.at[v])
        for v in range(out_ref.shape[0])
    ]
    for copy in copies:
        copy.start()
    for copy in copies:
        copy.wait()


def split_columns(amplitudes):
    pairs, rows, columns = amplitudes.shape
    owners = columns // LANES
    blocks = pl.pallas_call(
        split_kernel,
        in_specs=[pl.BlockSpec(memory_space=pltpu.VMEM)],
        out_specs=pl.BlockSpec(memory_space=pl.ANY),
        out_shape=pltpu.HBM((owners, pairs, rows, LANES), amplitudes.dtype),
        scratch_shapes=[pltpu.SemaphoreType.DMA((owners,))],
        compiler_params=params(8),
        cost_estimate=SMALL,
        name="split_columns",
    )(amplitudes)
    return blocks.reshape(owners, pairs * rows, LANES)


def half_kernel(first, place_ref, a_ref, *refs):
    out_ref, left_ref, panel, left_done, sems = refs[-5:]
    ranks = panel.shape[0]
    width = out_ref.shape[0] // ranks
    fetch = pltpu.make_async_copy(a_ref.at[pl.ds(first, left_ref.shape[0])], left_ref, left_done)
    fetch.start()
    fetch_parts(place_ref[0], refs[:-5], panel, sems)
    fetch.wait()
    for side in range(2):
        for back in range(ranks // 2):
            wait_block(place_ref[0], back, side, panel, sems)
    left = left_ref[...].reshape(out_ref.shape[1], left_ref.shape[2])
    for rank in range(ranks):
        result = lax.dot_general(
            left, panel[rank], (((1,), (1,)), ((), ())), preferred_element_type=jnp.float32
        ).astype(jnp.bfloat16)
        for j in range(width):
            out_ref[rank * width + j] = result[:, j * LANES : (j + 1) * LANES]


def half_ladder(amplitudes, own, other, first, count):
    anywhere = pl.BlockSpec(memory_space=pl.ANY)
    _, rows, depth = amplitudes.shape
    parts = [*own, *other]
    shape = (depth // LANES, count * rows, LANES)
    return pl.pallas_call(
        functools.partial(half_kernel, first),
        grid=(1,),
        in_specs=[pl.BlockSpec(memory_space=pltpu.SMEM)] + [anywhere] * (1 + len(parts)),
        out_specs=pl.BlockSpec(shape, lambda i: (0, 0, 0)),
        out_shape=jax.ShapeDtypeStruct(shape, jnp.bfloat16),
        scratch_shapes=[
            pltpu.VMEM((count, rows, depth), jnp.bfloat16),
            pltpu.VMEM(panel_shape(parts), jnp.bfloat16),
            pltpu.SemaphoreType.DMA,
            pltpu.SemaphoreType.DMA((len(own),)),
        ],
        compiler_params=params(60),
        cost_estimate=pl.CostEstimate(
            flops=2 * count * rows * depth * depth, bytes_accessed=depth * depth * 2, transcendentals=0
        ),
        name="half_ladder",
    )(lax.axis_index("pair").reshape(1), amplitudes, *parts)


def widen(source, target):
    owners = source.shape[0]
    rows = target.shape[1] // owners
    for q in range(target.shape[0]):
        for side in range(2):
            r = 2 * q + side
            target[q, :, side * LANES : (side + 1) * LANES] = source[
                :, r * rows : (r + 1) * rows, :
            ].reshape(owners * rows, LANES)


def finish(first, total, q, energy_ref, base_ref, screen_ref, out_ref):
    height = total.shape[0]
    for side in range(2):
        r = 2 * q + side
        screen = jnp.broadcast_to(
            screen_ref[r][:, None, :], (height // TILE, TILE, LANES)
        ).reshape(height, LANES)
        masked = total[:, side * LANES : (side + 1) * LANES] * screen
        out_ref[r] = (masked / (base_ref[...] - energy_ref[first + r])).astype(out_ref.dtype)


BACKS = (0, 1, 3, 2)


def back_of(step):
    return jnp.where(step == 2, 3, jnp.where(step == 3, 2, step))


def main_kernel(place_ref, energy_ref, a_ref, h_ref, base_ref, screen_ref, *refs):
    parts = len(PLACES) * 2
    k_parts, l_parts = refs[:parts], refs[parts : 2 * parts]
    out_ref, next_ref, ladder_ref, k_panel, l_panel, a_wide, h_wide, k_sems, l_sems, store_sems = refs[
        2 * parts :
    ]
    i = pl.program_id(0)
    pair = place_ref[0]
    chips = len(BACKS)

    @pl.when(i == 0)
    def _():
        for back in BACKS:
            fetch_parts(pair, k_parts, k_panel, k_sems, (back,))
            fetch_parts(pair, l_parts, l_panel, l_sems, (back,))
        widen(a_ref, a_wide)
        widen(h_ref, h_wide)

    def store(owner):
        return pltpu.make_async_copy(l_panel.at[owner], ladder_ref.at[owner], store_sems.at[owner])

    back = back_of(i)
    for side in range(2):
        wait_block(pair, back, side, k_panel, k_sems)
        wait_block(pair, back, side, l_panel, l_sems)
        store(owner_of(pair, back, side, chips)).start()
    rows = pl.ds(2 * chip_of(pair, back, chips), 2)
    k = k_panel[rows].reshape(HEIGHT, k_panel.shape[2])
    l = l_panel[rows].reshape(HEIGHT, l_panel.shape[2])
    ready = h_wide.shape[0]
    for q in range(a_wide.shape[0]):
        total = jnp.dot(k, a_wide[q], preferred_element_type=jnp.float32)
        if q < ready:
            total += jnp.dot(l, h_wide[q], preferred_element_type=jnp.float32)
            finish(0, total, q, energy_ref, base_ref, screen_ref, out_ref)
        else:
            next_ref[q - ready] = total

    @pl.when(i == pl.num_programs(0) - 1)
    def _():
        for owner in range(l_panel.shape[0]):
            store(owner).wait()


def ladder_kernel(
    first, cuts, energy_ref, l_hbm, h_ref, part_hbm, base_hbm, screen_ref, previous_ref, out_hbm,
    l_ref, part_ref, base_ref, out_ref, h_wide, sems, out_done,
):
    del previous_ref
    count = out_ref.shape[0]
    spans = [pl.ds(low, high - low) for low, high in zip(cuts, cuts[1:])]

    def loads(i):
        rows = spans[i]
        return [
            pltpu.make_async_copy(l_hbm.at[rows], l_ref.at[rows], sems.at[i, 0]),
            pltpu.make_async_copy(part_hbm.at[:, rows], part_ref.at[:, rows], sems.at[i, 1]),
            pltpu.make_async_copy(base_hbm.at[rows], base_ref.at[rows], sems.at[i, 2]),
        ]

    def store(i):
        rows = spans[i]
        return pltpu.make_async_copy(
            out_ref.at[:, rows], out_hbm.at[pl.ds(first, count), rows], out_done.at[i]
        )

    for i in range(2):
        for load in loads(i):
            load.start()
    widen(h_ref, h_wide)
    for i, rows in enumerate(spans):
        for load in loads(i):
            load.wait()
        if i + 2 < len(spans):
            for load in loads(i + 2):
                load.start()
        tiles = pl.ds(rows.start // TILE, rows.size // TILE)
        for q in range(h_wide.shape[0]):
            total = part_ref[q, rows] + jnp.dot(
                l_ref[rows], h_wide[q], preferred_element_type=jnp.float32
            )
            finish(
                first, total, q, energy_ref, base_ref.at[rows],
                screen_ref.at[pl.ds(first, count), tiles], out_ref.at[:, rows],
            )
        store(i).start()
    for i in range(len(spans)):
        store(i).wait()


HEIGHT = 512


def keep_in(space, values):
    return [pltpu.with_memory_space_constraint(value, space) for value in values]


def update_main(pair_energy, cycle_parts, ladder_parts, amps, half, base, screen):
    owners, height, _ = amps.shape
    pairs = pair_energy.shape[0]
    rows = height // pairs
    virt = owners * rows
    count = half.shape[1] // rows
    wide = [pltpu.VMEM((n // 2, virt, 2 * LANES), jnp.bfloat16) for n in (pairs, count)]
    anywhere = pl.BlockSpec(memory_space=pl.ANY)
    panel = panel_shape(cycle_parts)
    chips = len(BACKS)

    def chip(i, place):
        return chip_of(place[0], back_of(i), chips)

    grid_spec = pltpu.PrefetchScalarGridSpec(
        num_scalar_prefetch=1,
        grid=(chips,),
        in_specs=[
            pl.BlockSpec(memory_space=pltpu.SMEM),
            pl.BlockSpec(memory_space=pltpu.VMEM),
            pl.BlockSpec(memory_space=pltpu.VMEM),
            pl.BlockSpec((HEIGHT, LANES), lambda i, place: (chip(i, place), 0)),
            pl.BlockSpec((count, HEIGHT // TILE, LANES), lambda i, place: (0, chip(i, place), 0)),
        ]
        + [anywhere] * (len(cycle_parts) + len(ladder_parts)),
        out_specs=[
            pl.BlockSpec((count, HEIGHT, LANES), lambda i, place: (0, chip(i, place), 0)),
            pl.BlockSpec(
                ((pairs - count) // 2, HEIGHT, 2 * LANES), lambda i, place: (0, chip(i, place), 0)
            ),
            anywhere,
        ],
        scratch_shapes=[
            pltpu.VMEM(panel, jnp.bfloat16),
            pltpu.VMEM(panel, jnp.bfloat16),
            *wide,
        ]
        + [pltpu.SemaphoreType.DMA((panel[0],))] * 3,
    )
    return pl.pallas_call(
        main_kernel,
        grid_spec=grid_spec,
        out_shape=[
            jax.ShapeDtypeStruct((pairs, virt, LANES), jnp.bfloat16),
            pltpu.HBM(((pairs - count) // 2, virt, 2 * LANES), jnp.float32),
            pltpu.HBM(panel, jnp.bfloat16),
        ],
        compiler_params=params(40),
        cost_estimate=SMALL,
        name="update_main",
    )(
        lax.axis_index("pair").reshape(1), pair_energy, amps, half, base, screen,
        *keep_in(pltpu.HBM, cycle_parts), *keep_in(pltpu.HBM, ladder_parts),
    )


def update_ladder(pair_energy, ladder, half, part, base, screen, previous, first):
    owners = half.shape[0]
    virt = ladder.shape[0]
    count = half.shape[1] // (virt // owners)
    cuts = (0, HEIGHT // 2, *range(3 * HEIGHT // 2, virt, HEIGHT), virt)
    steps = len(cuts) - 1
    anywhere = pl.BlockSpec(memory_space=pl.ANY)
    whole = pl.BlockSpec(memory_space=pltpu.VMEM)
    return pl.pallas_call(
        functools.partial(ladder_kernel, first, cuts),
        in_specs=[
            pl.BlockSpec(memory_space=pltpu.SMEM),
            anywhere,
            whole,
            anywhere,
            anywhere,
            whole,
            anywhere,
        ],
        out_specs=anywhere,
        out_shape=jax.ShapeDtypeStruct(previous.shape, previous.dtype),
        scratch_shapes=[
            pltpu.VMEM(ladder.shape, jnp.bfloat16),
            pltpu.VMEM(part.shape, jnp.float32),
            pltpu.VMEM(base.shape, jnp.float32),
            pltpu.VMEM((count, virt, LANES), jnp.bfloat16),
            pltpu.VMEM((count // 2, virt, 2 * LANES), jnp.bfloat16),
            pltpu.SemaphoreType.DMA((steps, 3)),
            pltpu.SemaphoreType.DMA((steps,)),
        ],
        input_output_aliases={6: 0},
        compiler_params=params(28),
        cost_estimate=SMALL,
        name="update_ladder",
    )(
        pair_energy, *keep_in(pltpu.HBM, [ladder]), half, *keep_in(pltpu.HBM, [part]), base, screen,
        previous,
    )


def local(amplitudes, cycle_panel, ladder_panel, virt_energy, pair_energy, tile_mask):
    pairs = amplitudes.shape[0]
    count = pairs // CHUNKS
    exchange = functools.partial(
        lax.all_to_all, axis_name="virt", split_axis=0, concat_axis=0, tiled=True
    )
    after = lax.optimization_barrier
    v = lax.axis_index("virt")
    rows, columns = ladder_panel.shape
    owners = columns // LANES
    ranks = virt_energy.shape[0] // (owners * rows)

    def along(part, step):
        return lax.ppermute(part, "pair", z_shift(ranks, step))

    def across(parts):
        return [lax.ppermute(part, "pair", other_core(ranks)) for part in parts]

    def first_parts(top, bottom):
        return [along(top, 1), along(bottom, 3)]

    def last_parts(top, bottom, first):
        return [along(bottom, 1), along(top, 3), along(first[0], 1), along(first[1], 3)]

    with jax.named_scope("spread_panels"):
        both = jnp.concatenate([ladder_panel, cycle_panel])
        both = exchange(jnp.broadcast_to(both[None], (owners, 2 * rows, columns)))
        middle = owners // 2
        halves = [
            both[i * middle : (i + 1) * middle, j * rows : (j + 1) * rows].reshape(-1, columns)
            for j in range(2)
            for i in range(2)
        ]
        halves, own = after((halves, amplitudes))
        ladder_halves, cycle_halves = halves[:2], halves[2:]
    with jax.named_scope("exchange_amplitudes"):
        amps = exchange(split_columns(own))
    with jax.named_scope("update"):
        virt_energy, tile_mask, _ = after((virt_energy, tile_mask, halves))
        column_energy = lax.dynamic_slice_in_dim(virt_energy, v * LANES, LANES)
        base = virt_energy[:, None] + column_energy[None, :]
        screen = jnp.repeat(tile_mask.astype(jnp.float32), TILE, axis=2)
    with jax.named_scope("gather_ladder"):
        first = first_parts(*ladder_halves)
        other = across(ladder_halves)
        first, other = after((first, other))
        last = last_parts(*ladder_halves, first)
        other += across(first)
        last, cycle_halves = after((last, cycle_halves))
        mine, other = ladder_halves + first + last, other + across(last)
    with jax.named_scope("gather_cycle"):
        first = first_parts(*cycle_halves)
    with jax.named_scope("half_ladder"):
        sent = half_ladder(amplitudes, mine, other, 0, count)
        sent, first, own, amps, base, screen = after((sent, first, amplitudes, amps, base, screen))
        half = exchange(sent)
    with jax.named_scope("gather_cycle"):
        last = last_parts(*cycle_halves, first)
        close = across(cycle_halves + first)
    with jax.named_scope("half_ladder"):
        sent = half_ladder(own, mine, other, count, count)
        last, sent = after((last, sent))
        half_tail = exchange(sent)
    with jax.named_scope("gather_cycle"):
        cycle_parts = cycle_halves + first + last + close + across(last)
    with jax.named_scope("update"):
        out, part, ladder = update_main(
            pair_energy, cycle_parts, mine + other, amps, half, base, screen
        )
        ladder = ladder.reshape(-1, columns)
        return update_ladder(pair_energy, ladder, half_tail, part, base, screen, out, count)


def solution(mesh):
    in_specs = (
        P("pair", "virt", None),
        P(("pair", "virt"), None),
        P(("pair", "virt"), None),
        P(),
        P("pair"),
        P("pair", None, "virt"),
    )
    out_specs = P("pair", None, "virt")
    return jax.shard_map(local, mesh=mesh, in_specs=in_specs, out_specs=out_specs, check_vma=False)
```
